256 devices in a mesh: role: 2 (over z_lo), dp: 4 (over y), vocab: 32 (over z_hi, x, core).
Axes of the slice: x: 4, y: 4, z: 8 (z_hi: 4, z_lo: 2; z = z_hi * 2 + z_lo), core: 2. Of those that a mesh axis runs over, the one named last changes fastest.
Arguments:
- hidden: bfloat16 [4096, 1792], P(('role', 'dp'))
- out_weight: bfloat16 [1792, 77824], P(None, 'vocab')
- teacher_logits: bfloat16 [4096, 77824], P(('role', 'dp'), 'vocab')
- token_ids: int32 [4096], P(('role', 'dp')), may hold values from 0 to 77823
- loss_mask: int32 [4096], P(('role', 'dp')), may hold values from 0 to 1
Outputs:
- token_kl: float32 [4096], P(('role', 'dp'))
- chosen_logprob: float32 [4096], P(('role', 'dp'))
- grad_hidden: bfloat16 [4096, 1792], P(('role', 'dp', 'vocab'))
- grad_weight: bfloat16 [1792, 77824], P(('role', 'dp'), 'vocab')
The draws below stay inside these ranges and needn't reach their ends.
All inputs are finite; a program needn't handle non-finite values.
Results may differ from the reference program's by a relative error of at most 0.02.
Values may be sent and summed in bfloat16 or wider, within the bound.
A program may use at most 128 MiB of HBM per device.

```python
import jax
import jax.numpy as jnp
from jax import lax

H = 1792
TOK_DEV = 512
V = 77824
TOKENS = 4096


def base_weight(key):
    key = jax.random.fold_in(key, 71)
    scale_key, value_key = jax.random.split(key)
    column_scale = jnp.exp(jax.random.uniform(scale_key, (V,), jnp.float32, jnp.log(0.5), jnp.log(3.0)))
    values = jax.random.normal(value_key, (H, V), jnp.float32)
    return values * H ** (-0.5) * column_scale[None, :]


def draw_out_weight(key, part):
    return base_weight(key).astype(jnp.bfloat16)


def draw_hidden(key, part):
    key = jax.random.fold_in(key, 3)
    scale_key, value_key = jax.random.split(key, 2)
    row_scale = jnp.exp(jax.random.uniform(scale_key, (TOKENS,), jnp.float32, jnp.log(0.05), jnp.log(0.3)))
    result = jax.random.normal(value_key, (TOKENS, H), jnp.float32) * row_scale[:, None]
    return result.astype(jnp.bfloat16)


def draw_teacher_logits(key, part):
    key = jax.random.fold_in(key, 5)
    row_key, column_key, value_key = jax.random.split(key, 3)
    row_scale = jnp.exp(jax.random.uniform(row_key, (TOKENS,), jnp.float32, jnp.log(1.0), jnp.log(4.0)))
    column_scale = jnp.exp(jax.random.uniform(column_key, (V,), jnp.float32, jnp.log(0.8), jnp.log(3.0)))
    result = jax.random.normal(value_key, (TOKENS, V), jnp.float32) * row_scale[:, None] * column_scale[None, :]
    return result.astype(jnp.bfloat16)


def draw_loss_mask(key, part):
    key = jax.random.fold_in(key, 9)
    draws = jax.random.randint(key, (TOKENS,), 0, 1000)
    threshold = 250 + 650 * jnp.arange(TOKENS) // TOKENS
    return (draws < threshold).astype(jnp.int32)


def touch_ends(values, own_key, low, top_value):
    place = [jax.random.randint(jax.random.fold_in(own_key, axis), (), 0, length) for axis, length in enumerate(values.shape)]
    longest = values.shape.index(max(values.shape))
    neighbour = place[:longest] + [(place[longest] + 1) % values.shape[longest]] + place[longest + 1:]
    return values.at[tuple(place)].set(low).at[tuple(neighbour)].set(top_value)


def setup_inputs(seed: int = 0) -> dict:
    splits = jax.random.split(jax.random.key(seed), 6)
    hidden = draw_hidden(jax.random.fold_in(splits[5], 71), 0)
    out_weight = draw_out_weight(jax.random.fold_in(splits[5], 71), 0)
    teacher_logits = draw_teacher_logits(jax.random.fold_in(splits[5], 71), 0)
    token_ids = touch_ends(jax.random.randint(splits[3], (TOKENS,), 0, V), jax.random.fold_in(splits[3], 1), 0, V - 1).astype(jnp.int32)
    loss_mask = draw_loss_mask(jax.random.fold_in(splits[5], 71), 0)
    return {"hidden": hidden, "out_weight": out_weight, "teacher_logits": teacher_logits, "token_ids": token_ids, "loss_mask": loss_mask}


def reference(hidden, out_weight, teacher_logits, token_ids, loss_mask):
    teacher_all = jnp.roll(teacher_logits, TOKENS // 2, axis=0)
    mask_all = loss_mask.astype(jnp.float32)
    mask_total = jnp.maximum(jnp.sum(mask_all), 1.0)
    blocks = TOKENS // TOK_DEV
    hidden_blocks = hidden.reshape(blocks, TOK_DEV, H)
    teacher_blocks = teacher_all.reshape(blocks, TOK_DEV, V)
    id_blocks = token_ids.reshape(blocks, TOK_DEV)
    mask_blocks = mask_all.reshape(blocks, TOK_DEV)

    def step(weight_sum, inputs):
        rows, teacher_rows, ids_rows, mask_rows = inputs
        logits = jnp.dot(rows, out_weight, preferred_element_type=jnp.float32)
        teacher = teacher_rows.astype(jnp.float32)
        lse_student = jax.nn.logsumexp(logits, axis=1)
        lse_teacher = jax.nn.logsumexp(teacher, axis=1)
        log_student = logits - lse_student[:, None]
        log_teacher = teacher - lse_teacher[:, None]
        probs = jnp.exp(log_student)
        gap = log_student - log_teacher
        kl_rows = jnp.sum(probs * gap, axis=1)
        chosen = jnp.take_along_axis(log_student, ids_rows[:, None].astype(jnp.int32), axis=1)[:, 0]
        grad_logits = ((mask_rows / mask_total)[:, None] * probs * (gap - kl_rows[:, None])).astype(jnp.bfloat16)
        grad_rows = lax.dot_general(grad_logits, out_weight, (((1,), (1,)), ((), ())), preferred_element_type=jnp.float32).astype(jnp.bfloat16)
        weight_sum = weight_sum + lax.dot_general(rows, grad_logits, (((0,), (0,)), ((), ())), preferred_element_type=jnp.float32)
        return weight_sum, (kl_rows, chosen, grad_rows)

    weight_sum, outputs = lax.scan(step, jnp.zeros((H, V), jnp.float32), (hidden_blocks, teacher_blocks, id_blocks, mask_blocks))
    kl_rows, chosen, grad_rows = outputs
    return kl_rows.reshape(TOKENS), chosen.reshape(TOKENS), grad_rows.reshape(TOKENS, H), weight_sum.astype(jnp.bfloat16)
```

```python
import functools

import jax
import jax.numpy as jnp
from jax import lax
from jax.experimental import pallas as pl
from jax.experimental.pallas import tpu as pltpu
from jax.sharding import PartitionSpec as P

F32 = jnp.float32
BF16 = jnp.bfloat16
MESH = pl.DeviceIdType.MESH

TOK = 512
H = 1792
VW = 2432
LANE = 128
TILES = VW // LANE
NJ = 5
BLK = NJ * LANE
CH = 256
HALF = H // 2
ROWS = 224


def _rows(i, n):
    return pl.ds(pl.multiple_of(i * n, n), n)


def kernel_body(
    hidden, weight, teacher, ids, mask,
    kl_out, chosen_out, gh_out, gw_out,
    wv, tv, hall, first, rest, logits, lmax, sacc, tacc, idb, coef, gown, grecv,
    st1, st1r, st2, st2r, fin, fin_r, meta, meta_r, cnt, cnt_r,
    zs, zr, wacc, fs, idv, mkv, klv, chv, gh, gha, gb, gbr, gc, gcr, gd,
    lsem, ssem, rsem,
):
    r = lax.axis_index("role")
    d = lax.axis_index("dp")
    v = lax.axis_index("vocab")
    zh = lax.div(v, 8)
    x = lax.rem(lax.div(v, 2), 4)
    c = lax.rem(v, 2)

    def dev(r_, d_, zh_, x_, c_):
        return (r_, d_, (zh_ * 4 + x_) * 2 + c_)

    def plus(a, o):
        return lax.rem(a + o, 4)

    def along_z(o):
        z = lax.rem(zh * 2 + r + o, 8)
        return dev(lax.rem(z, 2), d, lax.div(z, 2), x, c)

    z_up, z_down = along_z(1), along_z(7)
    mate = dev(1 - r, d, zh, x, c)
    core = dev(r, d, zh, x, 1 - c)
    dp_peer = [None] + [dev(r, plus(d, o), zh, x, c) for o in (1, 2, 3)]
    x_peer = [None] + [dev(r, d, zh, plus(x, o), c) for o in (1, 2, 3)]
    zh_peer = [None] + [dev(r, d, plus(zh, o), x, c) for o in (1, 2, 3)]
    xc_peer = [None] + [dev(r, d, zh, plus(x, o), 1 - c) for o in (1, 2, 3)]

    count = [0]
    pending = []

    def remote(src, dst, to):
        i = count[0]
        count[0] += 1
        cp = pltpu.make_async_remote_copy(
            src_ref=src, dst_ref=dst, send_sem=ssem.at[i], recv_sem=rsem.at[i],
            device_id=to, device_id_type=MESH,
        )
        return cp

    def send(src, dst, to):
        cp = remote(src, dst, to)
        cp.start()
        pending.append(cp)
        return cp

    def sent(cps):
        for cp in cps:
            cp.wait_send()
            pending[:] = [q for q in pending if q is not cp]

    load_w = pltpu.make_async_copy(weight, wv, lsem.at[0])
    load_t = pltpu.make_async_copy(teacher, tv, lsem.at[1])
    load_i = pltpu.make_async_copy(ids, idv, lsem.at[2 + NJ])
    load_m = pltpu.make_async_copy(mask, mkv, lsem.at[3 + NJ])
    load_i.start()
    load_m.start()
    load_t.start()
    load_w.start()

    barrier = pltpu.get_barrier_semaphore()
    partners = [z_up, z_down, core] + dp_peer[1:] + x_peer[1:] + zh_peer[1:] + xc_peer[1:]
    for p in partners:
        pl.semaphore_signal(barrier, inc=1, device_id=p, device_id_type=MESH)
    load_i.wait()
    load_m.wait()
    meta[...] = jnp.concatenate(
        [mkv[...].astype(F32), idv[...].astype(F32), jnp.zeros((6, TOK), F32)], axis=0
    )
    pl.semaphore_wait(barrier, len(partners))

    def send_own(k):
        base = pl.multiple_of(k * CH + c * 128, 128)
        up = pl.ds(base, 64)
        down = pl.ds(pl.multiple_of(base + 64, 64), 64)
        return [
            send(hidden.at[up], hall.at[0, up], z_up),
            send(hidden.at[down], hall.at[0, down], z_down),
        ]

    meta_cp = send(meta, meta_r, mate)
    own = [send_own(0)]
    first_rows = hidden.at[pl.ds(pl.multiple_of(c * 128 + x * 32, 32), 32)]
    first_cp = [send(first_rows, first.at[o - 1], dp_peer[o]) for o in (1, 2, 3)]

    load_t.wait()

    def teacher_stats(i, _):
        rows = _rows(i, 64)
        m = tv[rows, 0:LANE]
        for j in range(1, TILES):
            m = jnp.maximum(m, tv[rows, j * LANE:(j + 1) * LANE])
        m = jnp.broadcast_to(jnp.max(m.astype(F32), axis=1, keepdims=True), (64, LANE))
        s = jnp.zeros((64, LANE), F32)
        for j in range(TILES):
            s = s + jnp.exp(tv[rows, j * LANE:(j + 1) * LANE].astype(F32) - m)
        tacc[0, rows, :] = m
        tacc[1, rows, :] = s
        return 0

    lax.fori_loop(0, TOK // 64, teacher_stats, 0)

    others = pl.ds(1, 3)

    def cross(cps, buf, row, n):
        for cp in cps:
            cp.wait_recv()
        out = []
        for i, to in enumerate((z_up, z_down)):
            rows = pl.ds(pl.multiple_of(row + i * n, n), n)
            out.append(send(buf.at[:, pl.ds(i * n, n)], hall.at[others, rows], to))
        return out

    rest_rows = hidden.at[pl.ds(pl.multiple_of(CH + c * 128 + 64, 64), 64)]
    rest_cp = [send(rest_rows, rest.at[o - 1], dp_peer[o]) for o in (1, 2, 3)]
    sent(own[0])
    own.append(send_own(1))

    meta_cp.wait_recv()
    both = meta[0:1, :] + meta_r[0:1, :]
    part = both[:, 0:128] + both[:, 128:256] + both[:, 256:384] + both[:, 384:512]
    cnt[...] = jnp.broadcast_to(part, (8, LANE))
    cnt_cp = [send(cnt, cnt_r.at[o - 1], dp_peer[o]) for o in (1, 2, 3)]
    id_cols = jnp.concatenate([meta_r[...], jnp.zeros((120, TOK), F32)], axis=0).T
    idb[...] = jnp.broadcast_to(id_cols[:, 1:2], (TOK, LANE)) - (v * VW).astype(F32)

    load_w.wait()

    def piece(k, x_):
        n = 32 if k == 0 else 16
        return pl.ds(pl.multiple_of(k * CH + c * 128 + x_ * n, 16), n)

    def core_rows(k):
        return pl.ds(pl.multiple_of(k * CH + c * 128, 128), 128)

    left_cols, right_cols = pl.ds(0, HALF), pl.ds(HALF, HALF)

    def core_own(k):
        for cp in own[k]:
            cp.wait_recv()
        fwd = send(hall.at[0, core_rows(k)], hall.at[0, core_rows(k)], core)
        if k == 0:
            return fwd, None
        mine = piece(k, x)
        return fwd, [send(hall.at[0, mine], hall.at[o, mine], dp_peer[o]) for o in (1, 2, 3)]

    def x_first(k, ys):
        for cp in ys:
            cp.wait_recv()
        mine = piece(k, x)
        return [
            send(hall.at[others, mine], hall.at[others, mine], x_peer[1]),
            send(hall.at[others, mine], hall.at[others, mine], x_peer[3]),
        ]

    def x_second(k, xs):
        out = []
        for cp, o, cols in zip(xs, (3, 1), (left_cols, right_cols)):
            cp.wait_recv()
            theirs = hall.at[others, piece(k, plus(x, o)), cols]
            out.append(send(theirs, theirs, x_peer[4 - o]))
        return out

    def forward_core(k, xs):
        for cp in xs:
            cp.wait_recv()
        rows = hall.at[others, core_rows(k)]
        return send(rows, rows, core)

    def logit_tile(k, first, width, start):
        rs = slice(k * CH, (k + 1) * CH)
        cols = pl.ds(first, width)
        l = jnp.dot(hall[0, rs, :], wv[:, cols], preferred_element_type=F32)
        logits[rs, cols] = l
        m = l[:, 0:LANE] if start else jnp.maximum(lmax[rs, :], l[:, 0:LANE])
        for q in range(1, width // LANE):
            m = jnp.maximum(m, l[:, q * LANE:(q + 1) * LANE])
        lmax[rs, :] = m

    def logits_chunk(k):
        logit_tile(k, 0, LANE, True)

        def body(n, _):
            logit_tile(k, pl.multiple_of(n * 768 + LANE, LANE), 768, False)
            return 0

        lax.fori_loop(0, 3, body, 0)

    def student_stats(k):
        def body(i, _):
            rows = pl.ds(pl.multiple_of(k * CH + i * 64, 64), 64)
            m = jnp.broadcast_to(jnp.max(lmax[rows, :], axis=1, keepdims=True), (64, LANE))
            token = idb[rows, :]
            lane = lax.broadcasted_iota(jnp.int32, (64, LANE), 1).astype(F32)
            s = jnp.zeros((64, LANE), F32)
            g = s
            picked = s
            for j in range(TILES):
                cols = slice(j * LANE, (j + 1) * LANE)
                l = logits[rows, cols]
                t = tv[rows, cols].astype(F32)
                e = jnp.exp(l - m)
                s = s + e
                g = g + e * (l - t)
                picked = picked + jnp.where(lane == token - float(j * LANE), l, 0.0)
            sacc[0, rows, :] = m
            sacc[1, rows, :] = s
            sacc[2, rows, :] = g
            sacc[3, rows, :] = picked
            return 0

        lax.fori_loop(0, CH // 64, body, 0)
        rs = slice(k * CH, (k + 1) * CH)

        def total(a):
            return jnp.sum(a.T, axis=0, keepdims=True)

        st1[k] = jnp.concatenate(
            [
                sacc[0, rs, :].T[0:1], total(sacc[1, rs, :]), total(sacc[2, rs, :]),
                total(sacc[3, rs, :]), tacc[0, rs, :].T[0:1], total(tacc[1, rs, :]),
                jnp.zeros((2, CH), F32),
            ],
            axis=0,
        )
        cps = [send(st1.at[k], st1r.at[k, 0], core)]
        for o in (1, 2, 3):
            cps.append(send(st1.at[k], st1r.at[k, o], x_peer[o]))
            cps.append(send(st1.at[k], st1r.at[k, 3 + o], xc_peer[o]))
        return cps

    def combine(msgs):
        top = functools.reduce(jnp.maximum, [m[0:1] for m in msgs])
        ttop = functools.reduce(jnp.maximum, [m[4:5] for m in msgs])
        s = g = pk = ts = None
        for m in msgs:
            w = jnp.exp(m[0:1] - top)
            tw = jnp.exp(m[4:5] - ttop)
            a, b, p, t = w * m[1:2], w * m[2:3], m[3:4], tw * m[5:6]
            s, g, pk, ts = (a, b, p, t) if s is None else (s + a, g + b, pk + p, ts + t)
        return top, s, g, pk, ttop, ts

    def stats_second(k, cps):
        for cp in cps:
            cp.wait_recv()
        rows = combine([st1[k]] + [st1r[k, i] for i in range(7)])
        st2[k] = jnp.concatenate(list(rows) + [jnp.zeros((2, CH), F32)], axis=0)
        return [send(st2.at[k], st2r.at[k, o - 1], zh_peer[o]) for o in (1, 2, 3)]

    def stats_final(k, cps):
        for cp in cps:
            cp.wait_recv()
        top, s, g, pk, ttop, ts = combine([st2[k]] + [st2r[k, i] for i in range(3)])
        lse = top + jnp.log(s)
        lse_t = ttop + jnp.log(ts)
        mean_gap = g / s
        rs = slice(k * CH, (k + 1) * CH)
        fin[k] = jnp.concatenate(
            [mean_gap - (lse - lse_t), pk - lse, jnp.zeros((6, CH), F32)], axis=0
        )
        scale = meta_r[0:1, rs] / mask_total
        cols = jnp.concatenate([lse, mean_gap, scale, jnp.zeros((125, CH), F32)], axis=0).T
        for i in range(3):
            coef[i, rs, :] = jnp.broadcast_to(cols[:, i:i + 1], (CH, LANE))
        return send(fin.at[k], fin_r.at[k], mate)

    def grad_tile(k, j):
        def body(i, _):
            rows = pl.ds(pl.multiple_of(k * CH + i * 64, 64), 64)
            lse, mean_gap, scale = coef[0, rows, :], coef[1, rows, :], coef[2, rows, :]
            for e in range(4):
                if e * NJ + j >= TILES:
                    continue
                cols = slice((e * NJ + j) * LANE, (e * NJ + j + 1) * LANE)
                l = logits[rows, cols]
                t = tv[rows, cols].astype(F32)
                grad = scale * jnp.exp(l - lse) * ((l - t) - mean_gap)
                gown[e, rows, j * LANE:(j + 1) * LANE] = grad.astype(BF16)
            return 0

        lax.fori_loop(0, CH // 64, body, 0)

    def g_copies(k, j):
        cps = []
        rs = pl.ds(0, TOK) if k is None else pl.ds(k * CH, CH)
        cs = pl.ds(j * LANE, LANE)
        for o in (1, 2, 3):
            e = plus(d, o)
            cps.append((remote(gown.at[e, rs, cs], grecv.at[o - 1, rs, cs], dp_peer[o]), e))
        return cps

    def g_each(u, what):
        for cp, e in gcp[u]:
            if u[1] < NJ - 1:
                getattr(cp, what)()
            else:
                pl.when(e < 3)(getattr(cp, what))

    def g_start(*u):
        gcp[u] = g_copies(*u)
        g_each(u, "start")

    def g_next(prev, u):
        g_each(prev, "wait_send")
        g_start(*u)

    def gh_chunk(k, first=0, last=H // 256):
        rs = slice(k * CH, (k + 1) * CH)

        def body(n, _):
            cols = _rows(n, 256)
            acc = None
            for e in range(4):
                width = min(BLK, VW - e * BLK)
                part_ = lax.dot_general(
                    gown[e, rs, 0:width], wv[cols, e * BLK:e * BLK + width],
                    (((1,), (1,)), ((), ())), preferred_element_type=F32,
                )
                acc = part_ if acc is None else acc + part_
            out = acc.astype(BF16)
            for u in range(16):
                w = k * 16 + u
                gh[w % 2, (w // 2) % 4, w // 8, :, cols] = out[u * 16:(u + 1) * 16]
            return 0

        lax.fori_loop(first, last, body, 0)

    fwd0, _ = core_own(0)
    cross0 = cross(first_cp, first, c * 128 + x * 32, 16)
    fwd0.wait_recv()
    logits_chunk(0)
    st1_0 = student_stats(0)
    xa0 = x_first(0, cross0)
    fwd1, ys1 = core_own(1)
    fwd1.wait_recv()
    logits_chunk(1)
    st1_1 = student_stats(1)
    st2_0 = stats_second(0, st1_0)
    xb0 = x_second(0, xa0)
    xa1 = x_first(1, ys1)
    for cp in cnt_cp:
        cp.wait_recv()
    mask_sum = cnt[...] + cnt_r[0] + cnt_r[1] + cnt_r[2]
    mask_total = jnp.maximum(jnp.sum(mask_sum[0:1], axis=1, keepdims=True), 1.0)
    st2_1 = stats_second(1, st1_1)
    last1 = cross(rest_cp, rest, CH + c * 128 + 64, 32)
    fin0 = stats_final(0, st2_0)
    gcp = {}
    grad_tile(0, 0)
    g_start(0, 0)
    grad_tile(0, 1)
    g_start(0, 1)
    for j in range(2, NJ):
        grad_tile(0, j)
    gh_chunk(0, 0, 6)
    fin1 = stats_final(1, st2_1)
    grad_tile(1, 0)
    g_start(1, 0)
    for j in range(1, NJ):
        grad_tile(1, j)
    cs0 = forward_core(0, xb0)
    xb1 = x_second(1, xa1)
    gh_chunk(0, 6, 7)
    g_start(1, 1)
    gh_chunk(1, 0, 5)
    cs1 = forward_core(1, xb1 + last1)
    gh_chunk(1, 5, 7)
    a_cp = send(gh.at[1 - c], gha, core)
    g_each((0, 0), "wait_send")
    g_next((1, 0), (None, 2))
    cs0.wait_recv()
    cs1.wait_recv()

    def weight_dot(half, j):
        cols = pl.ds(pl.multiple_of(half * HALF, LANE), HALF)
        cs = slice(j * LANE, (j + 1) * LANE)
        acc = None
        for o in range(4):
            g = gown[d, :, cs] if o == 0 else grecv[o - 1, :, cs]
            part_ = lax.dot_general(
                hall[o, :, cols], g, (((0,), (0,)), ((), ())), preferred_element_type=F32
            )
            acc = part_ if acc is None else acc + part_
        return acc

    def guarded(j, f):
        if j < NJ - 1:
            f()
        else:
            pl.when(d < 3)(f)

    def out_cols(j):
        d_ = d if j < NJ - 1 else lax.rem(d, 3)
        return pl.ds(pl.multiple_of(d_ * BLK + j * LANE, LANE), LANE)

    zcp = [remote(zs.at[j], zr.at[j], mate) for j in range(NJ)]
    fcp = [
        [
            remote(
                fs.at[j, plus(d, o)],
                gw_out.at[:, out_cols(j)],
                dp_peer[o],
            )
            for o in (1, 2, 3)
        ]
        for j in range(NJ)
    ]
    lcp = [
        pltpu.make_async_copy(
            fs.at[j, d],
            gw_out.at[:, out_cols(j)],
            lsem.at[2 + j],
        )
        for j in range(NJ)
    ]

    def weight_partial(j):
        def f():
            for u in ((0, j), (1, j)) if j < 2 else ((None, j),):
                for cp, _ in gcp[u]:
                    cp.wait_recv()
            zs[j] = weight_dot(1 - r, j).astype(BF16)
            if j > 0:
                zcp[j - 1].wait_send()
            zcp[j].start()
            wacc[j] = weight_dot(r, j)

        guarded(j, f)

    def weight_final(j):
        def f():
            zcp[j].wait_recv()
            for e in range(4):
                rs = slice(e * ROWS, (e + 1) * ROWS)
                fs[j, e] = (wacc[j, rs, :] + zr[j, rs, :].astype(F32)).astype(BF16)
            for cp in fcp[j]:
                cp.start()
            lcp[j].start()

        guarded(j, f)

    weight_partial(0)
    for k, cp in enumerate((fin0, fin1)):
        cp.wait_recv()
        rs = slice(k * CH, (k + 1) * CH)
        klv[:, rs] = fin_r[k, 0:1, :]
        chv[:, rs] = fin_r[k, 1:2, :]
    store_kl = pltpu.make_async_copy(klv, kl_out, lsem.at[4 + NJ])
    store_ch = pltpu.make_async_copy(chv, chosen_out, lsem.at[5 + NJ])
    store_kl.start()
    store_ch.start()
    a_cp.wait_recv()

    def add_a(i, _):
        gb[i] = (gh[c, i].astype(F32) + gha[i].astype(F32)).astype(BF16)
        return 0

    lax.fori_loop(0, 4, add_a, 0)
    b_cp = [send(gb.at[plus(x, o)], gbr.at[o - 1], x_peer[o]) for o in (1, 2, 3)]
    g_each((0, 1), "wait_send")
    g_next((1, 1), (None, 3))
    weight_partial(1)
    weight_final(0)
    g_next((None, 2), (None, 4))
    weight_partial(2)
    weight_final(1)
    for cp in b_cp:
        cp.wait_recv()
    for i in range(4):
        acc = gb[x, i].astype(F32)
        for o in range(3):
            acc = acc + gbr[o, i].astype(F32)
        gc[i] = acc.astype(BF16)
    c_cp = [send(gc.at[plus(zh, o)], gcr.at[o - 1], zh_peer[o]) for o in (1, 2, 3)]
    weight_partial(3)
    weight_final(2)
    weight_partial(4)
    weight_final(3)
    weight_final(4)
    for cp in c_cp:
        cp.wait_recv()
    acc = gc[zh].astype(F32)
    for o in range(3):
        acc = acc + gcr[o].astype(F32)
    gd[...] = acc.astype(BF16)
    d_cp = send(gd, gh_out, mate)

    d_cp.wait_recv()
    store_kl.wait()
    store_ch.wait()

    for cp in pending:
        cp.wait_send()
    for j in (3, 4):
        g_each((None, j), "wait_send")
    for j in range(NJ):
        def drain(j=j):
            if j == NJ - 1:
                zcp[j].wait_send()
            lcp[j].wait()
            for cp in fcp[j]:
                cp.wait_send()

        guarded(j, drain)
        if j == NJ - 2:
            pl.when(d == 3)(zcp[j].wait_send)
        for o in (1, 2, 3):
            if j < NJ - 1:
                fcp[j][o - 1].wait_recv()
            else:
                pl.when(plus(d, 4 - o) < 3)(fcp[j][o - 1].wait_recv)


N_COPIES = 140


def hand_on(a, b, c, d, a_out, b_out, c_out, d_out):
    a_out[...] = a[...]
    b_out[...] = b[...]
    c_out[...] = c[...]
    d_out[...] = d[...]


def local(hidden, out_weight, teacher_logits, token_ids, loss_mask):
    any_ = pl.BlockSpec(memory_space=pl.ANY)
    vm = pl.BlockSpec(memory_space=pltpu.VMEM)
    V = pltpu.VMEM
    outs = (
        jax.ShapeDtypeStruct((1, TOK), F32),
        jax.ShapeDtypeStruct((1, TOK), F32),
        jax.ShapeDtypeStruct((16, H), BF16),
        jax.ShapeDtypeStruct((ROWS, VW), BF16),
    )
    kl, chosen, grad_hidden, grad_weight = pl.pallas_call(
        kernel_body,
        out_shape=outs,
        in_specs=[any_] * 5,
        out_specs=(any_,) * 4,
        scratch_shapes=[
            V((H, VW), BF16),
            V((TOK, VW), BF16),
            V((4, TOK, H), BF16),
            V((3, 32, H), BF16),
            V((3, 64, H), BF16),
            V((TOK, VW), F32),
            V((TOK, LANE), F32),
            V((4, TOK, LANE), F32),
            V((2, TOK, LANE), F32),
            V((TOK, LANE), F32),
            V((3, TOK, LANE), F32),
            V((4, TOK, BLK), BF16),
            V((3, TOK, BLK), BF16),
            V((2, 8, CH), F32),
            V((2, 7, 8, CH), F32),
            V((2, 8, CH), F32),
            V((2, 3, 8, CH), F32),
            V((2, 8, CH), F32),
            V((2, 8, CH), F32),
            V((8, TOK), F32),
            V((8, TOK), F32),
            V((8, LANE), F32),
            V((3, 8, LANE), F32),
            V((NJ, HALF, LANE), BF16),
            V((NJ, HALF, LANE), BF16),
            V((NJ, HALF, LANE), F32),
            V((NJ, 4, ROWS, LANE), BF16),
            V((1, TOK), jnp.int32),
            V((1, TOK), jnp.int32),
            V((1, TOK), F32),
            V((1, TOK), F32),
            V((2, 4, 4, 16, H), BF16),
            V((4, 4, 16, H), BF16),
            V((4, 4, 16, H), BF16),
            V((3, 4, 16, H), BF16),
            V((4, 16, H), BF16),
            V((3, 16, H), BF16),
            V((16, H), BF16),
            pltpu.SemaphoreType.DMA((6 + NJ,)),
            pltpu.SemaphoreType.DMA((N_COPIES,)),
            pltpu.SemaphoreType.DMA((N_COPIES,)),
        ],
        compiler_params=pltpu.CompilerParams(
            collective_id=0, has_side_effects=True, vmem_limit_bytes=60 << 20
        ),
        cost_estimate=pl.CostEstimate(
            flops=6 * TOK * H * VW, bytes_accessed=16 << 20, transcendentals=3 * TOK * VW
        ),
        name="distill",
    )(hidden, out_weight, teacher_logits, token_ids.reshape(1, TOK), loss_mask.reshape(1, TOK))
    kl, chosen, grad_hidden, grad_weight = pl.pallas_call(
        hand_on,
        out_shape=outs,
        in_specs=[vm] * 4,
        out_specs=(vm,) * 4,
        name="handon",
    )(kl, chosen, grad_hidden, grad_weight)
    return kl.reshape(TOK), chosen.reshape(TOK), grad_hidden, grad_weight


def solution(mesh):
    return jax.shard_map(
        local,
        mesh=mesh,
        in_specs=(
            P(("role", "dp"), None),
            P(None, "vocab"),
            P(("role", "dp"), "vocab"),
            P(("role", "dp")),
            P(("role", "dp")),
        ),
        out_specs=(
            P(("role", "dp")),
            P(("role", "dp")),
            P(("role", "dp", "vocab"), None),
            P(("role", "dp"), "vocab"),
        ),
        check_vma=False,
    )
```
